128 devices in a mesh: gx: 16 (over y, z), gy: 8 (over x, core).
Axes of the slice: x: 4, y: 4, z: 4, core: 2. Of those that a mesh axis runs over, the one named last changes fastest.
Arguments:
- probes: bfloat16 [16, 131072], P(None, ('gx', 'gy')), may hold values from -73 to 73, as said below
- previous: bfloat16 [16, 131072], P(None, ('gx', 'gy')), may hold values from -6 to 6
- prev_coupling: float32 [16, 16], replicated, may hold values from -1.5 to 1.5
- leaves: bfloat16 [128, 1024, 1024], P(('gx', 'gy')), may hold values from -1 to 3, as said below
- bases: bfloat16 [7, 64, 131072], P(None, None, ('gx', 'gy')), may hold values from -6 to 6
- leaf_sizes: int32 [128], P(('gx', 'gy')), may hold values from 1 to 1024, 98304 in all
Outputs:
- rayleigh: float32 [16, 16], replicated
- factor: float32 [16, 16], replicated
- next_block: float32 [16, 131072], P(None, ('gx', 'gy'))
The draws below stay inside these ranges and needn't reach their ends.
Inputs may be any that keep to these rules, and one draw needn't show every extreme that they name: For every probe p and slot s, |probes[p, s]| stays within the range below. Each leaves[i] is symmetric. `leaf_sizes`: the real points of a leaf fill its first slots; the sizes sum to 98304.
All inputs are finite; a program needn't handle non-finite values. No bound on the sum of `leaf_sizes` on one device may be relied on, other than what follows from the above.
Results may differ from the reference program's by a relative error of at most 0.0022.
Values sent between devices are 32-bit elements; how exact they have to be, the bound alone decides.
No kernel may reach another device: no remote copies, remote signals or barrier semaphores. Data moves between devices by JAX's collectives and lax.ppermute only.
A program may use at most 64 MiB of HBM per device.

```python
import math
import jax
import jax.numpy as jnp
import numpy as np
from jax import lax

LEAF = 1024
RANK = 64
PROBES = 16
LEAVES = 128
NPTS = 131072
LEVELS = 7
FILLED = 98304


def draw_probes(key, part):
    base_key = jax.random.fold_in(key, 17)
    first, second, third = jax.random.split(base_key, 3)
    values = jax.random.truncated_normal(first, -4.0, 4.0, (PROBES, NPTS), jnp.float32)
    rows = 10.0 ** (jax.random.uniform(second, (NPTS,), jnp.float32) - 0.5)
    columns = 10.0 ** (jax.random.uniform(third, (PROBES,), jnp.float32) - 0.5)
    rising = 0.6 * (1.0 + 2.0 * jnp.arange(NPTS, dtype=jnp.float32) / NPTS)
    return (values * (rows * rising)[None, :] * columns[:, None]).astype(jnp.bfloat16)


def draw_leaves(key, part):
    base_key = jax.random.fold_in(key, 29)

    def one_leaf(index):
        leaf_key = jax.random.fold_in(base_key, index)
        raw = jax.random.truncated_normal(leaf_key, -4.0, 4.0, (LEAF, LEAF), jnp.float32)
        symmetric = (raw + raw.T) * (0.5 / LEAF ** 0.5)
        return (symmetric + 2.0 * jnp.eye(LEAF, dtype=jnp.float32)).astype(jnp.bfloat16)
    return lax.map(one_leaf, jnp.arange(LEAVES, dtype=jnp.int32))


def block_levels(stream_key, dims, cuts, low, high):
    def one(dim, shards_of):
        draws = jax.random.uniform(jax.random.fold_in(jax.random.fold_in(stream_key, 6), dim), (shards_of,), jnp.float32, low / len(cuts), high / len(cuts))
        return jnp.repeat(jnp.exp(draws), dims[dim] // shards_of).reshape((-1,) + (1,) * (len(dims) - dim - 1))

    level = one(*cuts[0])
    for cut in cuts[1:]:
        level = level * one(*cut)
    return level


def split_up(count, total, most, skew):
    weights = [(1 << 20) // math.isqrt(standing ** skew) + 1 for standing in range(2, count + 1)]
    rest, given = total - most - (count - 1), [1] * (count - 1)
    while rest > 0:
        movable = [i for i in range(count - 1) if given[i] < most]
        mass, budget = sum([weights[i] for i in movable]), rest
        for i in movable:
            extra = min(most - given[i], max(1, budget * weights[i] // mass), rest)
            given[i] = given[i] + extra
            rest = rest - extra
    return np.array([most] + given)


def ragged_sizes(key, count, total, bound, lean):
    if count == 2:
        one = jax.random.randint(key, (), max(1, total - bound), min(bound, total - 1) + 1)
        return jnp.stack([one, total - one])
    lengths = jnp.asarray(split_up(count, total, bound, lean), jnp.int32)
    twos = (count - 1) // 2
    source_of, taker = lengths[1:1 + 2 * twos:2], lengths[2:2 + 2 * twos:2]
    margin = jnp.minimum(source_of - 1, bound - taker)
    passed = jax.random.randint(jax.random.fold_in(key, 1), (twos,), 0, 1 << 20) % (margin + 1)
    lengths = lengths.at[1:1 + 2 * twos:2].set(source_of - passed).at[2:2 + 2 * twos:2].set(taker + passed)
    return lengths[jax.random.permutation(jax.random.fold_in(key, 2), count)]


def centred(stream_key, dims, scale, most, shards=(), kind=jnp.bfloat16):
    drawn = jax.random.normal(stream_key, dims, jnp.float32) * scale
    if len(shards) > 0:
        drawn = block_levels(stream_key, dims, shards, -0.22, 0.18) * drawn
    return jnp.clip(drawn, min=-most, max=most).astype(kind)


def setup_inputs(seed: int = 0) -> dict:
    seeds = jax.random.split(jax.random.key(seed), 7)
    return {
        "probes": draw_probes(jax.random.fold_in(seeds[6], 71), 0),
        "previous": centred(seeds[1], (PROBES, NPTS), 1.0, 6.0, ((1, 128),)),
        "prev_coupling": centred(seeds[2], (PROBES, PROBES), PROBES ** -0.5, 1.5, (), jnp.float32),
        "leaves": draw_leaves(jax.random.fold_in(seeds[6], 71), 0),
        "bases": centred(seeds[4], (LEVELS, RANK, NPTS), 1.0, 6.0, ((2, 128),)),
        "leaf_sizes": ragged_sizes(seeds[5], LEAVES, FILLED, LEAF, 1).astype(jnp.int32),
    }


def reference(probes, previous, prev_coupling, leaves, bases, leaf_sizes):
    highest = lax.Precision.HIGHEST
    valid = (jnp.arange(LEAF, dtype=jnp.int32)[None, :] < leaf_sizes[:, None]).reshape(NPTS)
    block = jnp.where(valid[None, :], probes, jnp.zeros_like(probes)).astype(jnp.float32)
    older = jnp.where(valid[None, :], previous, jnp.zeros_like(previous)).astype(jnp.float32)
    shaped = block.reshape(PROBES, LEAVES // 8, 8, LEAF).transpose(1, 2, 0, 3)
    grouped = leaves.reshape(LEAVES // 8, 8, LEAF, LEAF)

    def apply_group(pair):
        mats, vecs = pair
        return jnp.einsum('lrc,lpc->lpr', mats.astype(jnp.float32), vecs, precision=highest)
    image = lax.map(apply_group, (grouped, shaped))
    image = image.transpose(2, 0, 1, 3).reshape(PROBES, NPTS)
    for level in range(LEVELS):
        width = LEAF * 2 ** level
        nodes = NPTS // width
        basis = bases[level].astype(jnp.float32).reshape(RANK, nodes, width)
        pieces = block.reshape(PROBES, nodes, width)
        coef = jnp.einsum('pnm,rnm->pnr', pieces, basis, precision=highest)
        partner = coef.reshape(PROBES, nodes // 2, 2, RANK)[:, :, ::-1, :].reshape(PROBES, nodes, RANK)
        partner = (partner * (1.0 / math.sqrt(RANK * width))).astype(jnp.bfloat16).astype(jnp.float32)
        image = image + jnp.einsum('pnr,rnm->pnm', partner, basis, precision=highest).reshape(PROBES, NPTS)
    image = jnp.where(valid[None, :], image, jnp.zeros_like(image))
    inverse = 1.0 / FILLED
    rayleigh = jnp.dot(block, image.T, precision=highest) * inverse
    residual = image - jnp.dot(rayleigh.T, block, precision=highest) - jnp.dot(prev_coupling, older, precision=highest)
    gram = jnp.dot(residual, residual.T, precision=highest) * inverse
    factor = jnp.linalg.cholesky(gram)
    next_block = jax.scipy.linalg.solve_triangular(factor, residual, lower=True)
    return (rayleigh, factor, next_block)
```

```python
import math

import jax
import jax.numpy as jnp
from jax import lax
from jax.sharding import Mesh
from jax.sharding import PartitionSpec as P

AXES = ("gx_0", "gx_1", "gy_0", "gy_1")
CHIPS = ("gx_0", "gx_1", "gy_0")
CORE = "gy_1"
HIGHEST = lax.Precision.HIGHEST


def fold(m):
    half = m.shape[-2] // 2
    return jnp.concatenate([m[..., :half, :], m[..., half:, :]], -1)


def unfold(m):
    half = m.shape[-1] // 2
    return jnp.concatenate([m[..., :half], m[..., half:]], -2)


def body(probes, previous, prev_coupling, leaves, bases, leaf_sizes):
    probe_count = probes.shape[0]
    rows = leaves.shape[1]
    rank = bases.shape[1]
    levels = bases.shape[0]
    chips = lax.axis_size(CHIPS)
    chip_bits = chips.bit_length() - 1
    devices = lax.axis_size(AXES)
    inverse = 1.0 / (devices * rows * 3 // 4)
    chip = lax.axis_index(CHIPS)
    valid = (jnp.arange(rows, dtype=jnp.int32) < leaf_sizes[0])[None, :]
    block = jnp.where(valid, probes, jnp.zeros_like(probes))
    older = jnp.where(valid, previous, jnp.zeros_like(previous))
    partials = jnp.einsum("pm,krm->kpr", block, bases, preferred_element_type=jnp.float32)
    partials = fold(partials)
    other = lax.ppermute(partials, CORE, [(0, 1), (1, 0)])
    image = jnp.einsum("rc,pc->pr", leaves[0], block, preferred_element_type=jnp.float32)
    mine = partials + other
    send = jnp.zeros((chips,) + mine.shape[1:], jnp.float32)
    apart = chip ^ jnp.arange(chips, dtype=jnp.int32)
    for bit in range(chip_bits):
        here = ((apart >> bit) == 1)[:, None, None]
        send = jnp.where(here, mine[bit + 1][None], send)
    got = lax.all_to_all(send, CHIPS, 0, 0, tiled=True)
    partners = [other[0]]
    for bit in range(chip_bits):
        first = ((chip >> bit) ^ 1) << bit
        partners.append(lax.dynamic_slice_in_dim(got, first, 1 << bit, 0).sum(0))
    scaled = [
        unfold(partners[level] * (1.0 / math.sqrt(rank * rows * 2**level))).astype(jnp.bfloat16)
        for level in range(levels)
    ]
    image = image + jnp.einsum(
        "kpr,krm->pm", jnp.stack(scaled), bases, preferred_element_type=jnp.float32
    )
    image = jnp.where(valid, image, jnp.zeros_like(image))
    dense = block.astype(jnp.float32)
    shifted = image - jnp.dot(prev_coupling, older.astype(jnp.float32), precision=HIGHEST)
    left = jnp.concatenate([shifted, dense], 0)
    right = jnp.concatenate([shifted, dense, image], 0)
    sums = jnp.dot(left, right.T, precision=HIGHEST)
    p = probe_count
    packed = jnp.concatenate(
        [sums[:p, :p], sums[p:, :p], sums[p:, p : 2 * p], sums[p:, 2 * p :]], 1
    )
    packed = fold(packed)
    packed = packed + lax.ppermute(packed, CORE, [(0, 1), (1, 0)])
    spread = jnp.broadcast_to(packed[None], (chips,) + packed.shape)
    total = unfold(lax.all_to_all(spread, CHIPS, 0, 0, tiled=True).sum(0)) * inverse
    shifted_shifted, block_shifted, block_block, rayleigh = jnp.split(total, 4, 1)
    cross = jnp.dot(rayleigh.T, block_shifted, precision=HIGHEST)
    inner = jnp.dot(rayleigh.T, block_block, precision=HIGHEST)
    gram = shifted_shifted - cross - cross.T + jnp.dot(inner, rayleigh, precision=HIGHEST)
    residual = shifted - jnp.dot(rayleigh.T, dense, precision=HIGHEST)
    factor = jnp.linalg.cholesky(gram)
    next_block = jax.scipy.linalg.solve_triangular(factor, residual, lower=True)
    return (rayleigh, factor, next_block)


def solution(mesh):
    split = Mesh(mesh.devices.reshape(4, 4, 4, 2), AXES)
    return jax.shard_map(
        body,
        mesh=split,
        in_specs=(
            P(None, AXES),
            P(None, AXES),
            P(),
            P(AXES, None, None),
            P(None, None, AXES),
            P(AXES),
        ),
        out_specs=(P(), P(), P(None, AXES)),
        check_vma=False,
    )
```

```python
import functools
import math

import jax
import jax.numpy as jnp
from jax import lax
from jax.experimental import pallas as pl
from jax.experimental.pallas import tpu as pltpu
from jax.sharding import Mesh
from jax.sharding import PartitionSpec as P

AXES = ("gx_0", "gx_1", "gy_0", "gy_1")
CHIPS = ("gx_0", "gx_1", "gy_0")
CORE = "gy_1"
HIGHEST = lax.Precision.HIGHEST
VMEM = pl.BlockSpec(memory_space=pltpu.VMEM)
SMEM = pl.BlockSpec(memory_space=pltpu.SMEM)
HBM = pl.BlockSpec(memory_space=pltpu.HBM)
LIMIT = 32 * 1024 * 1024
FIRST_LIMIT = 55200 * 1024
F32 = jnp.float32
LANES = 128


def fold(m):
    half = m.shape[-2] // 2
    return jnp.concatenate([m[..., :half, :], m[..., half:, :]], -1)


def unfold(m):
    half = m.shape[-1] // 2
    return jnp.concatenate([m[..., :half], m[..., half:]], -2)


def contract(a, b, over, precision=None):
    return lax.dot_general(
        a, b, ((over[:1], over[1:]), ((), ())), precision=precision, preferred_element_type=F32
    )


def call(kernel, outs, ins, scratch=(), flops=0, moved=0, limit=LIMIT):
    return pl.pallas_call(
        kernel,
        out_shape=outs,
        in_specs=ins,
        out_specs=jax.tree.map(lambda _: VMEM, outs),
        scratch_shapes=list(scratch),
        compiler_params=pltpu.CompilerParams(vmem_limit_bytes=limit),
        cost_estimate=pl.CostEstimate(flops=flops, bytes_accessed=moved, transcendentals=0),
    )


def masked(sizes, raw):
    slot = lax.broadcasted_iota(jnp.int32, raw.shape, 1)
    return jnp.where(slot < sizes[0], raw.astype(F32), 0.0)


def coefficients(sizes, probes_hbm, bases_hbm, out_ref, probes, bases, sems):
    levels, rank, rows = bases.shape
    copies = [
        pltpu.make_async_copy(probes_hbm, probes, sems.at[0]),
        pltpu.make_async_copy(bases_hbm, bases, sems.at[1]),
    ]
    for copy in copies:
        copy.start()
    for copy in copies:
        copy.wait()
    block = masked(sizes, probes[...]).astype(probes.dtype)
    both = contract(block, bases[...].reshape(levels * rank, rows), (1, 1))
    for t in range(levels):
        out_ref[t] = fold(both[:, t * rank : (t + 1) * rank])


def chip_index():
    index = 0
    for axis in CHIPS:
        index = index * lax.axis_size(axis) + lax.axis_index(axis)
    return index


def outgoing(chip_bits, chip_ref, own, other, out_ref):
    chip = chip_ref[0]
    out_ref[chip] = jnp.zeros(own.shape[1:], F32)
    for bit in range(chip_bits):
        first = ((chip >> bit) ^ 1) << bit
        mine = own[bit + 1] + other[bit + 1]
        out_ref[pl.ds(first, 1 << bit)] = jnp.broadcast_to(mine[None], (1 << bit,) + mine.shape)


def coupled(chip_bits, chip_ref, sizes, got, other, bases, image, pull, block, shifted_ref, sums_ref):
    levels, rank, rows = bases.shape
    dense = block[...].astype(F32)
    chip = chip_ref[0]
    partners = [other[0]]
    for bit in range(chip_bits):
        first = ((chip >> bit) ^ 1) << bit
        partners.append(jnp.sum(got[pl.ds(first, 1 << bit)], axis=0))
    scaled = [
        unfold(partners[t] * (1.0 / math.sqrt(rank * rows * 2**t))) for t in range(levels)
    ]
    weights = jnp.concatenate(scaled, 1).astype(bases.dtype)
    far = contract(weights, bases[...].reshape(levels * rank, rows), (1, 0))
    full = masked(sizes, image[...] + far)
    shifted = full - pull[...]
    shifted_ref[...] = shifted
    corner = contract(shifted, shifted, (1, 1), HIGHEST)
    lower = contract(dense, jnp.concatenate([shifted, dense, full], 0), (1, 1), HIGHEST)
    sums_ref[...] = fold(jnp.concatenate([lower, corner], 1))


def last_part(inverse, got, shifted, block, rayleigh_ref, factor_ref, next_ref):
    total = unfold(jnp.sum(got[...], axis=0)) * inverse
    p = total.shape[0]
    block_shifted = total[:, :p]
    block_block = total[:, p : 2 * p]
    rayleigh = total[:, 2 * p : 3 * p]
    corner = total[:, 3 * p :]
    rayleigh_ref[...] = rayleigh
    right = contract(block_block, rayleigh, (1, 0), HIGHEST) - block_shifted
    gram = corner + contract(
        jnp.concatenate([rayleigh, -block_shifted], 0),
        jnp.concatenate([right, rayleigh], 0),
        (0, 0),
        HIGHEST,
    )
    residual = shifted[...] - contract(rayleigh, block[...].astype(F32), (0, 0), HIGHEST)
    starts = range(0, residual.shape[1], LANES)
    parts = [residual[:, at : at + LANES] for at in starts]
    row = lax.broadcasted_iota(jnp.int32, (p, LANES), 0)
    lane = lax.broadcasted_iota(jnp.int32, (p, LANES), 1)
    columns = [jnp.broadcast_to(gram[:, k : k + 1], (p, LANES)) for k in range(p)]
    factor = jnp.zeros((p, LANES), F32)
    scale = jnp.zeros((p, LANES), F32)
    for k in range(p):
        pivot = jnp.broadcast_to(columns[k][k : k + 1, :], (p, LANES))
        root = lax.rsqrt(pivot)
        ratio = jnp.where(row > k, columns[k], 0.0) * (1.0 / pivot)
        factor = jnp.where(lane == k, jnp.where(row >= k, columns[k], 0.0) * root, factor)
        scale = jnp.where(row == k, root, scale)
        for j in range(k + 1, p):
            columns[j] = columns[j] - ratio * columns[j][k : k + 1, :]
        parts = [part - ratio * part[k : k + 1, :] for part in parts]
    factor_ref[...] = factor[:, :p]
    for at, part in zip(starts, parts):
        next_ref[:, at : at + LANES] = part * scale


def body(probes, previous, prev_coupling, leaves, bases, leaf_sizes):
    probe_count = probes.shape[0]
    levels, rank, rows = bases.shape
    chips = lax.axis_size(CHIPS)
    chip_bits = chips.bit_length() - 1
    devices = lax.axis_size(AXES)
    inverse = 1.0 / (devices * rows * 3 // 4)
    chip = chip_index().astype(jnp.int32).reshape(1)
    swap = [(0, 1), (1, 0)]
    tile = (probe_count // 2, 2 * rank)
    wide = jax.ShapeDtypeStruct((probe_count, rows), F32)
    square = jax.ShapeDtypeStruct((probe_count, probe_count), F32)
    partials = call(
        coefficients,
        jax.ShapeDtypeStruct((levels,) + tile, F32),
        [SMEM, HBM, HBM],
        [
            pltpu.VMEM(probes.shape, probes.dtype),
            pltpu.VMEM(bases.shape, bases.dtype),
            pltpu.SemaphoreType.DMA((2,)),
        ],
        limit=FIRST_LIMIT,
    )(leaf_sizes, probes, bases)
    other = lax.ppermute(partials, CORE, swap)
    valid = (jnp.arange(rows, dtype=jnp.int32) < leaf_sizes[0])[None, :]
    block = jnp.where(valid, probes, jnp.zeros_like(probes))
    older = jnp.where(valid, previous, jnp.zeros_like(previous)).astype(F32)
    image = contract(block, leaves[0], (1, 0))
    pull = contract(prev_coupling, older, (1, 0), HIGHEST)
    other, image, pull, block = lax.optimization_barrier((other, image, pull, block))
    send = call(
        functools.partial(outgoing, chip_bits),
        jax.ShapeDtypeStruct((chips,) + tile, F32),
        [SMEM, VMEM, VMEM],
    )(chip, partials, other)
    got = lax.all_to_all(send, CHIPS, 0, 0, tiled=True)
    shifted, sums = call(
        functools.partial(coupled, chip_bits),
        (wide, jax.ShapeDtypeStruct((probe_count // 2, 8 * probe_count), F32)),
        [SMEM] * 2 + [VMEM] * 6,
    )(chip, leaf_sizes, got, other, bases, image, pull, block)
    sums = sums + lax.ppermute(sums, CORE, swap)
    spread = jnp.broadcast_to(sums[None], (chips,) + sums.shape)
    total = lax.all_to_all(spread, CHIPS, 0, 0, tiled=True)
    return call(
        functools.partial(last_part, inverse),
        (square, square, wide),
        [VMEM] * 3,
    )(total, shifted, block)


def solution(mesh):
    split = Mesh(mesh.devices.reshape(4, 4, 4, 2), AXES)
    return jax.shard_map(
        body,
        mesh=split,
        in_specs=(
            P(None, AXES),
            P(None, AXES),
            P(),
            P(AXES, None, None),
            P(None, None, AXES),
            P(AXES),
        ),
        out_specs=(P(), P(), P(None, AXES)),
        check_vma=False,
    )
```

```python
import functools
import math

import jax
import jax.numpy as jnp
from jax import lax
from jax.experimental import pallas as pl
from jax.experimental.pallas import tpu as pltpu
from jax.sharding import Mesh
from jax.sharding import PartitionSpec as P

AXES = ("gx_0", "gx_1", "gy_0", "gy_1")
CHIPS = ("gx_0", "gx_1", "gy_0")
CORE = "gy_1"
HIGHEST = lax.Precision.HIGHEST
VMEM = pl.BlockSpec(memory_space=pltpu.VMEM)
SMEM = pl.BlockSpec(memory_space=pltpu.SMEM)
HBM = pl.BlockSpec(memory_space=pltpu.HBM)
LIMIT = 32 * 1024 * 1024
FIRST_LIMIT = 55150 * 1024
F32 = jnp.float32
LANES = 128


def fold(m):
    half = m.shape[-2] // 2
    return jnp.concatenate([m[..., :half, :], m[..., half:, :]], -1)


def unfold(m):
    half = m.shape[-1] // 2
    return jnp.concatenate([m[..., :half], m[..., half:]], -2)


def contract(a, b, over, precision=None):
    return lax.dot_general(
        a, b, ((over[:1], over[1:]), ((), ())), precision=precision, preferred_element_type=F32
    )


def split(x, dtype):
    parts = []
    for _ in range(3):
        parts.append(x.astype(dtype))
        x = x - parts[-1].astype(F32)
    return parts


def gather(x, size, axis):
    parts = [lax.slice_in_dim(x, at, at + size, axis=axis) for at in (2 * size, size, 0)]
    return parts[0] + parts[1] + parts[2]


def call(kernel, outs, ins, scratch=(), flops=0, moved=0, limit=LIMIT):
    return pl.pallas_call(
        kernel,
        out_shape=outs,
        in_specs=ins,
        out_specs=jax.tree.map(lambda _: VMEM, outs),
        scratch_shapes=list(scratch),
        compiler_params=pltpu.CompilerParams(vmem_limit_bytes=limit),
        cost_estimate=pl.CostEstimate(flops=flops, bytes_accessed=moved, transcendentals=0),
    )


def masked(sizes, raw):
    slot = lax.broadcasted_iota(jnp.int32, raw.shape, 1)
    return jnp.where(slot < sizes[0], raw.astype(F32), 0.0)


def coefficients(sizes, probes_hbm, bases_hbm, out_ref, block_ref, probes, bases, sems):
    levels, rank, rows = bases.shape
    copies = [
        pltpu.make_async_copy(probes_hbm, probes, sems.at[0]),
        pltpu.make_async_copy(bases_hbm, bases, sems.at[1]),
    ]
    for copy in copies:
        copy.start()
    copies[0].wait()
    block = masked(sizes, probes[...]).astype(probes.dtype)
    block_ref[...] = block
    copies[1].wait()
    both = contract(block, bases[...].reshape(levels * rank, rows), (1, 1))
    for t in range(levels):
        out_ref[t] = fold(both[:, t * rank : (t + 1) * rank])


def chip_index():
    index = 0
    for axis in CHIPS:
        index = index * lax.axis_size(axis) + lax.axis_index(axis)
    return index


def outgoing(chip_bits, chip_ref, own, other, out_ref):
    chip = chip_ref[0]
    out_ref[chip] = jnp.zeros(own.shape[1:], F32)
    for bit in range(chip_bits):
        first = ((chip >> bit) ^ 1) << bit
        mine = own[bit + 1] + other[bit + 1]
        out_ref[pl.ds(first, 1 << bit)] = jnp.broadcast_to(mine[None], (1 << bit,) + mine.shape)


def coupled(chip_bits, chip_ref, sizes, got, other, bases, image, pull, block, shifted_ref, sums_ref):
    levels, rank, rows = bases.shape
    chip = chip_ref[0]
    partners = [other[0]]
    for bit in range(chip_bits):
        first = ((chip >> bit) ^ 1) << bit
        partners.append(jnp.sum(got[pl.ds(first, 1 << bit)], axis=0))
    scaled = [
        unfold(partners[t] * (1.0 / math.sqrt(rank * rows * 2**t))) for t in range(levels)
    ]
    weights = jnp.concatenate(scaled, 1).astype(bases.dtype)
    far = contract(weights, bases[...].reshape(levels * rank, rows), (1, 0))
    full = masked(sizes, image[...] + far)
    shifted = full - pull[...]
    shifted_ref[...] = shifted
    p = full.shape[0]
    parts = split(shifted, bases.dtype) + [block[...]] + split(full, bases.dtype)
    sums = contract(jnp.concatenate(parts[:4], 0), jnp.concatenate(parts, 0), (1, 1))
    corner = gather(sums[: 3 * p, : 3 * p], p, 0)
    lower = sums[3 * p :]
    pieces = [
        gather(lower[:, : 3 * p], p, 1),
        lower[:, 3 * p : 4 * p],
        gather(lower[:, 4 * p :], p, 1),
        gather(corner, p, 1),
    ]
    sums_ref[...] = fold(jnp.concatenate(pieces, 1))


def last_part(inverse, got, shifted, block, rayleigh_ref, factor_ref, next_ref):
    total = unfold(jnp.sum(got[...], axis=0)) * inverse
    p = total.shape[0]
    block_shifted = total[:, :p]
    block_block = total[:, p : 2 * p]
    rayleigh = total[:, 2 * p : 3 * p]
    corner = total[:, 3 * p :]
    rayleigh_ref[...] = rayleigh
    right = contract(block_block, rayleigh, (1, 0), HIGHEST) - block_shifted
    gram = corner + contract(
        jnp.concatenate([rayleigh, -block_shifted], 0),
        jnp.concatenate([right, rayleigh], 0),
        (0, 0),
        HIGHEST,
    )
    residual = shifted[...] - contract(rayleigh, block[...].astype(F32), (0, 0), HIGHEST)
    starts = range(0, residual.shape[1], LANES)
    parts = [residual[:, at : at + LANES] for at in starts]
    row = lax.broadcasted_iota(jnp.int32, (p, LANES), 0)
    lane = lax.broadcasted_iota(jnp.int32, (p, LANES), 1)
    columns = [jnp.broadcast_to(gram[:, k : k + 1], (p, LANES)) for k in range(p)]
    factor = jnp.zeros((p, LANES), F32)
    scale = jnp.zeros((p, LANES), F32)
    for k in range(p):
        pivot = jnp.broadcast_to(columns[k][k : k + 1, :], (p, LANES))
        root = lax.rsqrt(pivot)
        ratio = jnp.where(row > k, columns[k], 0.0) * (1.0 / pivot)
        factor = jnp.where(lane == k, jnp.where(row >= k, columns[k], 0.0) * root, factor)
        scale = jnp.where(row == k, root, scale)
        for j in range(k + 1, p):
            columns[j] = columns[j] - ratio * columns[j][k : k + 1, :]
        parts = [part - ratio * part[k : k + 1, :] for part in parts]
    factor_ref[...] = factor[:, :p]
    for at, part in zip(starts, parts):
        next_ref[:, at : at + LANES] = part * scale


def body(probes, previous, prev_coupling, leaves, bases, leaf_sizes):
    probe_count = probes.shape[0]
    levels, rank, rows = bases.shape
    chips = lax.axis_size(CHIPS)
    chip_bits = chips.bit_length() - 1
    devices = lax.axis_size(AXES)
    inverse = 1.0 / (devices * rows * 3 // 4)
    chip = chip_index().astype(jnp.int32).reshape(1)
    swap = [(0, 1), (1, 0)]
    tile = (probe_count // 2, 2 * rank)
    wide = jax.ShapeDtypeStruct((probe_count, rows), F32)
    square = jax.ShapeDtypeStruct((probe_count, probe_count), F32)
    partials, block = call(
        coefficients,
        (
            jax.ShapeDtypeStruct((levels,) + tile, F32),
            jax.ShapeDtypeStruct(probes.shape, probes.dtype),
        ),
        [SMEM, HBM, HBM],
        [
            pltpu.VMEM(probes.shape, probes.dtype),
            pltpu.VMEM(bases.shape, bases.dtype),
            pltpu.SemaphoreType.DMA((2,)),
        ],
        limit=FIRST_LIMIT,
    )(leaf_sizes, probes, bases)
    other = lax.ppermute(partials, CORE, swap)
    valid = (jnp.arange(rows, dtype=jnp.int32) < leaf_sizes[0])[None, :]
    older = jnp.where(valid, previous, jnp.zeros_like(previous)).astype(F32)
    image = contract(block, leaves[0], (1, 0))
    pull = contract(prev_coupling, older, (1, 0), HIGHEST)
    other, image, pull = lax.optimization_barrier((other, image, pull))
    send = call(
        functools.partial(outgoing, chip_bits),
        jax.ShapeDtypeStruct((chips,) + tile, F32),
        [SMEM, VMEM, VMEM],
    )(chip, partials, other)
    got = lax.all_to_all(send, CHIPS, 0, 0, tiled=True)
    shifted, sums = call(
        functools.partial(coupled, chip_bits),
        (wide, jax.ShapeDtypeStruct((probe_count // 2, 8 * probe_count), F32)),
        [SMEM] * 2 + [VMEM] * 6,
    )(chip, leaf_sizes, got, other, bases, image, pull, block)
    sums = sums + lax.ppermute(sums, CORE, swap)
    spread = jnp.broadcast_to(sums[None], (chips,) + sums.shape)
    total = lax.all_to_all(spread, CHIPS, 0, 0, tiled=True)
    return call(
        functools.partial(last_part, inverse),
        (square, square, wide),
        [VMEM] * 3,
    )(total, shifted, block)


def solution(mesh):
    split = Mesh(mesh.devices.reshape(4, 4, 4, 2), AXES)
    return jax.shard_map(
        body,
        mesh=split,
        in_specs=(
            P(None, AXES),
            P(None, AXES),
            P(),
            P(AXES, None, None),
            P(None, None, AXES),
            P(AXES),
        ),
        out_specs=(P(), P(), P(None, AXES)),
        check_vma=False,
    )
```

```python
import functools
import math

import jax
import jax.numpy as jnp
from jax import lax
from jax.experimental import pallas as pl
from jax.experimental.pallas import tpu as pltpu
from jax.sharding import Mesh
from jax.sharding import PartitionSpec as P

AXES = ("gx_0", "gx_1", "gy_0", "gy_1")
CHIPS = ("gx_0", "gx_1", "gy_0")
CORE = "gy_1"
HIGHEST = lax.Precision.HIGHEST
VMEM = pl.BlockSpec(memory_space=pltpu.VMEM)
SMEM = pl.BlockSpec(memory_space=pltpu.SMEM)
HBM = pl.BlockSpec(memory_space=pltpu.HBM)
LIMIT = 32 * 1024 * 1024
FIRST_LIMIT = 55150 * 1024
F32 = jnp.float32
LANES = 128


def fold(m):
    half = m.shape[-2] // 2
    return jnp.concatenate([m[..., :half, :], m[..., half:, :]], -1)


def unfold(m):
    half = m.shape[-1] // 2
    return jnp.concatenate([m[..., :half], m[..., half:]], -2)


def contract(a, b, over, precision=None):
    return lax.dot_general(
        a, b, ((over[:1], over[1:]), ((), ())), precision=precision, preferred_element_type=F32
    )


def split(x, dtype):
    parts = []
    for _ in range(3):
        parts.append(x.astype(dtype))
        x = x - parts[-1].astype(F32)
    return parts


def gather(x, size, axis):
    parts = [lax.slice_in_dim(x, at, at + size, axis=axis) for at in (2 * size, size, 0)]
    return parts[0] + parts[1] + parts[2]


def call(kernel, outs, ins, scratch=(), flops=0, moved=0, limit=LIMIT):
    return pl.pallas_call(
        kernel,
        out_shape=outs,
        in_specs=ins,
        out_specs=jax.tree.map(lambda _: VMEM, outs),
        scratch_shapes=list(scratch),
        compiler_params=pltpu.CompilerParams(vmem_limit_bytes=limit),
        cost_estimate=pl.CostEstimate(flops=flops, bytes_accessed=moved, transcendentals=0),
    )


def masked(sizes, raw):
    slot = lax.broadcasted_iota(jnp.int32, raw.shape, 1)
    return jnp.where(slot < sizes[0], raw.astype(F32), 0.0)


def keep_mask(sizes, keep_ref):
    slot = lax.broadcasted_iota(jnp.int32, keep_ref.shape, 1)
    keep_ref[...] = jnp.where(slot < sizes[0], 1.0, 0.0)


def coefficients(keep, probes, bases, out_ref, block_ref):
    levels, rank, rows = bases.shape
    block = jnp.where(keep[:1] > 0.0, probes[...].astype(F32), 0.0).astype(probes.dtype)
    block_ref[...] = block
    both = contract(block, bases[...].reshape(levels * rank, rows), (1, 1))
    for t in range(levels):
        out_ref[t] = fold(both[:, t * rank : (t + 1) * rank])


def chip_index():
    index = 0
    for axis in CHIPS:
        index = index * lax.axis_size(axis) + lax.axis_index(axis)
    return index


def outgoing(chip_bits, chip_ref, own, other, out_ref):
    chip = chip_ref[0]
    out_ref[chip] = jnp.zeros(own.shape[1:], F32)
    for bit in range(chip_bits):
        first = ((chip >> bit) ^ 1) << bit
        mine = own[bit + 1] + other[bit + 1]
        out_ref[pl.ds(first, 1 << bit)] = jnp.broadcast_to(mine[None], (1 << bit,) + mine.shape)


def coupled(chip_bits, chip_ref, sizes, got, other, bases, image, pull, block, shifted_ref, sums_ref):
    levels, rank, rows = bases.shape
    chip = chip_ref[0]
    partners = [other[0]]
    for bit in range(chip_bits):
        first = ((chip >> bit) ^ 1) << bit
        partners.append(jnp.sum(got[pl.ds(first, 1 << bit)], axis=0))
    scaled = [
        unfold(partners[t] * (1.0 / math.sqrt(rank * rows * 2**t))) for t in range(levels)
    ]
    weights = jnp.concatenate(scaled, 1).astype(bases.dtype)
    far = contract(weights, bases[...].reshape(levels * rank, rows), (1, 0))
    full = image[...] + far
    shifted = masked(sizes, full - pull[...])
    shifted_ref[...] = shifted
    p = full.shape[0]
    parts = split(shifted, bases.dtype) + [block[...]] + split(full, bases.dtype)
    sums = contract(jnp.concatenate(parts[:4], 0), jnp.concatenate(parts, 0), (1, 1))
    corner = gather(sums[: 3 * p, : 3 * p], p, 0)
    lower = sums[3 * p :]
    pieces = [
        gather(lower[:, : 3 * p], p, 1),
        lower[:, 3 * p : 4 * p],
        gather(lower[:, 4 * p :], p, 1),
        gather(corner, p, 1),
    ]
    sums_ref[...] = fold(jnp.concatenate(pieces, 1))


def last_part(inverse, got, shifted, block, rayleigh_ref, factor_ref, next_ref):
    total = unfold(jnp.sum(got[...], axis=0)) * inverse
    p = total.shape[0]
    block_shifted = total[:, :p]
    block_block = total[:, p : 2 * p]
    rayleigh = total[:, 2 * p : 3 * p]
    corner = total[:, 3 * p :]
    rayleigh_ref[...] = rayleigh
    right = contract(block_block, rayleigh, (1, 0), HIGHEST) - block_shifted
    gram = corner + contract(
        jnp.concatenate([rayleigh, -block_shifted], 0),
        jnp.concatenate([right, rayleigh], 0),
        (0, 0),
        HIGHEST,
    )
    residual = shifted[...] - contract(rayleigh, block[...].astype(F32), (0, 0), HIGHEST)
    starts = range(0, residual.shape[1], LANES)
    parts = [residual[:, at : at + LANES] for at in starts]
    row = lax.broadcasted_iota(jnp.int32, (p, LANES), 0)
    lane = lax.broadcasted_iota(jnp.int32, (p, LANES), 1)
    columns = [jnp.broadcast_to(gram[:, k : k + 1], (p, LANES)) for k in range(p)]
    factor = jnp.zeros((p, LANES), F32)
    scale = jnp.zeros((p, LANES), F32)
    for k in range(p):
        pivot = jnp.broadcast_to(columns[k][k : k + 1, :], (p, LANES))
        root = lax.rsqrt(pivot)
        ratio = jnp.where(row > k, columns[k], 0.0) * (1.0 / pivot)
        factor = jnp.where(lane == k, jnp.where(row >= k, columns[k], 0.0) * root, factor)
        scale = jnp.where(row == k, root, scale)
        for j in range(k + 1, p):
            columns[j] = columns[j] - ratio * columns[j][k : k + 1, :]
        parts = [part - ratio * part[k : k + 1, :] for part in parts]
    factor_ref[...] = factor[:, :p]
    for at, part in zip(starts, parts):
        next_ref[:, at : at + LANES] = part * scale


def body(probes, previous, prev_coupling, leaves, bases, leaf_sizes):
    probe_count = probes.shape[0]
    levels, rank, rows = bases.shape
    chips = lax.axis_size(CHIPS)
    chip_bits = chips.bit_length() - 1
    devices = lax.axis_size(AXES)
    inverse = 1.0 / (devices * rows * 3 // 4)
    chip = chip_index().astype(jnp.int32).reshape(1)
    swap = [(0, 1), (1, 0)]
    tile = (probe_count // 2, 2 * rank)
    wide = jax.ShapeDtypeStruct((probe_count, rows), F32)
    square = jax.ShapeDtypeStruct((probe_count, probe_count), F32)
    keep = call(
        keep_mask,
        jax.ShapeDtypeStruct((8, rows), F32),
        [SMEM],
        flops=1000000000,
        moved=0,
    )(leaf_sizes)
    partials, block = call(
        coefficients,
        (
            jax.ShapeDtypeStruct((levels,) + tile, F32),
            jax.ShapeDtypeStruct(probes.shape, probes.dtype),
        ),
        [VMEM] * 3,
        flops=2 * probe_count * levels * rank * rows,
        moved=2 * levels * rank * rows,
    )(keep, probes, bases)
    other = lax.ppermute(partials, CORE, swap)
    image = contract(block, leaves[0], (1, 0))
    pull = contract(prev_coupling, previous.astype(F32), (1, 0), HIGHEST)
    other, image, pull = lax.optimization_barrier((other, image, pull))
    send = call(
        functools.partial(outgoing, chip_bits),
        jax.ShapeDtypeStruct((chips,) + tile, F32),
        [SMEM, VMEM, VMEM],
    )(chip, partials, other)
    got = lax.all_to_all(send, CHIPS, 0, 0, tiled=True)
    shifted, sums = call(
        functools.partial(coupled, chip_bits),
        (wide, jax.ShapeDtypeStruct((probe_count // 2, 8 * probe_count), F32)),
        [SMEM] * 2 + [VMEM] * 6,
    )(chip, leaf_sizes, got, other, bases, image, pull, block)
    sums = sums + lax.ppermute(sums, CORE, swap)
    spread = jnp.broadcast_to(sums[None], (chips,) + sums.shape)
    total = lax.all_to_all(spread, CHIPS, 0, 0, tiled=True)
    return call(
        functools.partial(last_part, inverse),
        (square, square, wide),
        [VMEM] * 3,
    )(total, shifted, block)


def solution(mesh):
    split = Mesh(mesh.devices.reshape(4, 4, 4, 2), AXES)
    return jax.shard_map(
        body,
        mesh=split,
        in_specs=(
            P(None, AXES),
            P(None, AXES),
            P(),
            P(AXES, None, None),
            P(None, None, AXES),
            P(AXES),
        ),
        out_specs=(P(), P(), P(None, AXES)),
        check_vma=False,
    )
```

```python
import functools
import math

import jax
import jax.numpy as jnp
from jax import lax
from jax.experimental import pallas as pl
from jax.experimental.pallas import tpu as pltpu
from jax.sharding import Mesh
from jax.sharding import PartitionSpec as P

AXES = ("gx_0", "gx_1", "gy_0", "gy_1")
CHIPS = ("gx_0", "gx_1", "gy_0")
CORE = "gy_1"
HIGHEST = lax.Precision.HIGHEST
VMEM = pl.BlockSpec(memory_space=pltpu.VMEM)
SMEM = pl.BlockSpec(memory_space=pltpu.SMEM)
LIMIT = 32 * 1024 * 1024
F32 = jnp.float32
LANES = 128


def fold(m):
    half = m.shape[-2] // 2
    return jnp.concatenate([m[..., :half, :], m[..., half:, :]], -1)


def unfold(m):
    half = m.shape[-1] // 2
    return jnp.concatenate([m[..., :half], m[..., half:]], -2)


def contract(a, b, over, precision=None):
    return lax.dot_general(
        a, b, ((over[:1], over[1:]), ((), ())), precision=precision, preferred_element_type=F32
    )


def split(x, dtype):
    parts = []
    for _ in range(3):
        parts.append(x.astype(dtype))
        x = x - parts[-1].astype(F32)
    return parts


def call(kernel, outs, ins, scratch=(), flops=0, moved=0):
    return pl.pallas_call(
        kernel,
        out_shape=outs,
        in_specs=ins,
        out_specs=jax.tree.map(lambda _: VMEM, outs),
        scratch_shapes=list(scratch),
        compiler_params=pltpu.CompilerParams(vmem_limit_bytes=LIMIT),
        cost_estimate=pl.CostEstimate(flops=flops, bytes_accessed=moved, transcendentals=0),
    )


def masked(sizes, raw):
    slot = lax.broadcasted_iota(jnp.int32, raw.shape, 1)
    return jnp.where(slot < sizes[0], raw.astype(F32), 0.0)


def keep_mask(sizes, keep_ref):
    slot = lax.broadcasted_iota(jnp.int32, keep_ref.shape, 1)
    keep_ref[...] = jnp.where(slot < sizes[0], 1.0, 0.0)


def coefficients(keep, probes, bases, out_ref, block_ref):
    levels, rank, rows = bases.shape
    block = jnp.where(keep[:1] > 0.0, probes[...].astype(F32), 0.0).astype(probes.dtype)
    block_ref[...] = block
    both = contract(block, bases[...].reshape(levels * rank, rows), (1, 1))
    for t in range(levels):
        out_ref[t] = fold(both[:, t * rank : (t + 1) * rank])


def own_part(block, leaf, previous, coupling, image_ref, pull_ref):
    image_ref[...] = contract(block[...], leaf[0], (1, 0))
    pull_ref[...] = contract(coupling[...], previous[...].astype(F32), (1, 0), HIGHEST)


def chip_index():
    index = 0
    for axis in CHIPS:
        index = index * lax.axis_size(axis) + lax.axis_index(axis)
    return index


def outgoing(chip_bits, chip_ref, own, other, out_ref):
    chip = chip_ref[0]
    out_ref[chip] = jnp.zeros(own.shape[1:], F32)
    for bit in range(chip_bits):
        first = ((chip >> bit) ^ 1) << bit
        mine = own[bit + 1] + other[bit + 1]
        out_ref[pl.ds(first, 1 << bit)] = jnp.broadcast_to(mine[None], (1 << bit,) + mine.shape)


def coupled(chip_bits, chip_ref, sizes, got, other, bases, image, pull, block, shifted_ref, sums_ref):
    levels, rank, rows = bases.shape
    chip = chip_ref[0]
    partners = [other[0]]
    for bit in range(chip_bits):
        first = ((chip >> bit) ^ 1) << bit
        partners.append(jnp.sum(got[pl.ds(first, 1 << bit)], axis=0))
    tiles = [partners[t] * (1.0 / math.sqrt(rank * rows * 2**t)) for t in range(levels)]
    low = lax.broadcasted_iota(jnp.int32, tiles[0].shape, 1) < rank
    tiles += [jnp.zeros_like(tiles[0])] * (levels % 2)
    turned = [pltpu.roll(tile, rank, 1) for tile in tiles]
    pairs = range(0, levels, 2)
    upper = jnp.concatenate([jnp.where(low, tiles[t], turned[t + 1]) for t in pairs], 1)
    lower = jnp.concatenate([jnp.where(low, turned[t], tiles[t + 1]) for t in pairs], 1)
    weights = jnp.concatenate([upper, lower], 0)[:, : levels * rank].astype(bases.dtype)
    far = contract(weights, bases[...].reshape(levels * rank, rows), (1, 0))
    full = image[...] + far
    shifted = masked(sizes, full - pull[...])
    shifted_ref[...] = shifted
    p = full.shape[0]
    half = p // 2
    shifted_parts = split(shifted, bases.dtype)
    full_parts = split(full, bases.dtype)
    left = jnp.concatenate([block[...]] + shifted_parts, 0)
    sums = jnp.zeros((4 * p, LANES), F32)
    for i in (2, 1, 0):
        own = block[...] if i == 0 else jnp.zeros_like(block[...])
        right = [shifted_parts[i], own, full_parts[i], shifted_parts[i]]
        sums = sums + contract(left, jnp.concatenate(right + right, 0), (1, 1))
    with_block = sums[:p]
    with_shifted = (sums[3 * p :] + sums[2 * p : 3 * p]) + sums[p : 2 * p]
    lane = lax.broadcasted_iota(jnp.int32, (half, LANES), 1)
    side = LANES // 2
    upper = jnp.where(lane < 3 * p, with_block[:half], with_shifted[:half])
    lower = jnp.where(lane < side + 3 * p, with_block[half:], with_shifted[half:])
    sums_ref[...] = jnp.where(lane < side, upper, lower)


def last_part(inverse, got, shifted, block, rayleigh_ref, factor_ref, next_ref):
    total = unfold(jnp.sum(got[...], axis=0)) * inverse
    p = total.shape[0]
    block_shifted = total[:, :p]
    block_block = total[:, p : 2 * p]
    rayleigh = total[:, 2 * p : 3 * p]
    corner = total[:, 3 * p :]
    rayleigh_ref[...] = rayleigh
    right = contract(block_block, rayleigh, (1, 0), HIGHEST) - block_shifted
    gram = corner + contract(
        jnp.concatenate([rayleigh, -block_shifted], 0),
        jnp.concatenate([right, rayleigh], 0),
        (0, 0),
        HIGHEST,
    )
    residual = shifted[...] - contract(rayleigh, block[...].astype(F32), (0, 0), HIGHEST)
    starts = range(0, residual.shape[1], LANES)
    parts = [residual[:, at : at + LANES] for at in starts]
    row = lax.broadcasted_iota(jnp.int32, (p, LANES), 0)
    lane = lax.broadcasted_iota(jnp.int32, (p, LANES), 1)
    columns = [jnp.broadcast_to(gram[:, k : k + 1], (p, LANES)) for k in range(p)]
    factor = jnp.zeros((p, LANES), F32)
    scale = jnp.zeros((p, LANES), F32)
    for k in range(p):
        pivot = jnp.broadcast_to(columns[k][k : k + 1, :], (p, LANES))
        root = lax.rsqrt(pivot)
        ratio = jnp.where(row > k, columns[k], 0.0) * (1.0 / pivot)
        factor = jnp.where(lane == k, jnp.where(row >= k, columns[k], 0.0) * root, factor)
        scale = jnp.where(row == k, root, scale)
        for j in range(k + 1, p):
            columns[j] = columns[j] - ratio * columns[j][k : k + 1, :]
        parts = [part - ratio * part[k : k + 1, :] for part in parts]
    factor_ref[...] = factor[:, :p]
    for at, part in zip(starts, parts):
        next_ref[:, at : at + LANES] = part * scale


def body(probes, previous, prev_coupling, leaves, bases, leaf_sizes):
    probe_count = probes.shape[0]
    levels, rank, rows = bases.shape
    chips = lax.axis_size(CHIPS)
    chip_bits = chips.bit_length() - 1
    devices = lax.axis_size(AXES)
    inverse = 1.0 / (devices * rows * 3 // 4)
    chip = chip_index().astype(jnp.int32).reshape(1)
    swap = [(0, 1), (1, 0)]
    tile = (probe_count // 2, 2 * rank)
    wide = jax.ShapeDtypeStruct((probe_count, rows), F32)
    square = jax.ShapeDtypeStruct((probe_count, probe_count), F32)
    keep = call(
        keep_mask,
        jax.ShapeDtypeStruct((8, rows), F32),
        [SMEM],
        flops=1000000000,
        moved=0,
    )(leaf_sizes)
    partials, block = call(
        coefficients,
        (
            jax.ShapeDtypeStruct((levels,) + tile, F32),
            jax.ShapeDtypeStruct(probes.shape, probes.dtype),
        ),
        [VMEM] * 3,
        flops=2 * probe_count * levels * rank * rows,
        moved=2 * levels * rank * rows,
    )(keep, probes, bases)
    other = lax.ppermute(partials, CORE, swap)
    image, pull = call(
        own_part,
        (wide, wide),
        [VMEM] * 4,
        flops=2 * probe_count * rows * rows,
        moved=2 * rows * rows,
    )(block, leaves, previous, prev_coupling)
    other, image, pull = lax.optimization_barrier((other, image, pull))
    send = call(
        functools.partial(outgoing, chip_bits),
        jax.ShapeDtypeStruct((chips,) + tile, F32),
        [SMEM, VMEM, VMEM],
    )(chip, partials, other)
    got = lax.all_to_all(send, CHIPS, 0, 0, tiled=True)
    shifted, sums = call(
        functools.partial(coupled, chip_bits),
        (wide, jax.ShapeDtypeStruct((probe_count // 2, 8 * probe_count), F32)),
        [SMEM] * 2 + [VMEM] * 6,
    )(chip, leaf_sizes, got, other, bases, image, pull, block)
    sums = sums + lax.ppermute(sums, CORE, swap)
    spread = jnp.broadcast_to(sums[None], (chips,) + sums.shape)
    total = lax.all_to_all(spread, CHIPS, 0, 0, tiled=True)
    return call(
        functools.partial(last_part, inverse),
        (square, square, wide),
        [VMEM] * 3,
    )(total, shifted, block)


def solution(mesh):
    split = Mesh(mesh.devices.reshape(4, 4, 4, 2), AXES)
    return jax.shard_map(
        body,
        mesh=split,
        in_specs=(
            P(None, AXES),
            P(None, AXES),
            P(),
            P(AXES, None, None),
            P(None, None, AXES),
            P(AXES),
        ),
        out_specs=(P(), P(), P(None, AXES)),
        check_vma=False,
    )
```

```python
import functools
import math

import jax
import jax.numpy as jnp
from jax import lax
from jax.experimental import pallas as pl
from jax.experimental.pallas import tpu as pltpu
from jax.sharding import Mesh
from jax.sharding import PartitionSpec as P

AXES = ("gx_0", "gx_1", "gy_0", "gy_1")
CHIPS = ("gx_0", "gx_1", "gy_0")
CORE = "gy_1"
HIGHEST = lax.Precision.HIGHEST
VMEM = pl.BlockSpec(memory_space=pltpu.VMEM)
SMEM = pl.BlockSpec(memory_space=pltpu.SMEM)
LIMIT = 32 * 1024 * 1024
F32 = jnp.float32
LANES = 128


def fold(m):
    half = m.shape[-2] // 2
    return jnp.concatenate([m[..., :half, :], m[..., half:, :]], -1)


def unfold(m):
    half = m.shape[-1] // 2
    return jnp.concatenate([m[..., :half], m[..., half:]], -2)


def contract(a, b, over, precision=None):
    return lax.dot_general(
        a, b, ((over[:1], over[1:]), ((), ())), precision=precision, preferred_element_type=F32
    )


def split(x, dtype):
    parts = []
    for _ in range(3):
        parts.append(x.astype(dtype))
        x = x - parts[-1].astype(F32)
    return parts


def call(kernel, outs, ins, scratch=(), flops=0, moved=0):
    return pl.pallas_call(
        kernel,
        out_shape=outs,
        in_specs=ins,
        out_specs=jax.tree.map(lambda _: VMEM, outs),
        scratch_shapes=list(scratch),
        compiler_params=pltpu.CompilerParams(vmem_limit_bytes=LIMIT),
        cost_estimate=pl.CostEstimate(flops=flops, bytes_accessed=moved, transcendentals=0),
    )


def masked(sizes, raw):
    slot = lax.broadcasted_iota(jnp.int32, raw.shape, 1)
    return jnp.where(slot < sizes[0], raw.astype(F32), 0.0)


def keep_mask(sizes, keep_ref):
    slot = lax.broadcasted_iota(jnp.int32, keep_ref.shape, 1)
    keep_ref[...] = jnp.where(slot < sizes[0], 1.0, 0.0)


def coefficients(keep, probes, bases, out_ref, block_ref):
    levels, rank, rows = bases.shape
    block = jnp.where(keep[:1] > 0.0, probes[...].astype(F32), 0.0).astype(probes.dtype)
    block_ref[...] = block
    both = contract(block, bases[...].reshape(levels * rank, rows), (1, 1))
    for t in range(levels):
        out_ref[t] = fold(both[:, t * rank : (t + 1) * rank])


def own_part(block, leaf, previous, coupling, image_ref, pull_ref):
    image_ref[...] = contract(block[...], leaf[0], (1, 0))
    pull_ref[...] = contract(coupling[...], previous[...].astype(F32), (1, 0), HIGHEST)


def chip_index():
    index = 0
    for axis in CHIPS:
        index = index * lax.axis_size(axis) + lax.axis_index(axis)
    return index


def outgoing(chip_bits, chip_ref, own, other, out_ref):
    chip = chip_ref[0]
    out_ref[chip] = jnp.zeros(own.shape[1:], F32)
    for bit in range(chip_bits):
        first = ((chip >> bit) ^ 1) << bit
        mine = own[bit + 1] + other[bit + 1]
        out_ref[pl.ds(first, 1 << bit)] = jnp.broadcast_to(mine[None], (1 << bit,) + mine.shape)


def coupled(chip_bits, chip_ref, sizes, got, other, bases, image, pull, block, shifted_ref, sums_ref):
    levels, rank, rows = bases.shape
    chip = chip_ref[0]
    partners = [other[0]]
    for bit in range(chip_bits):
        first = ((chip >> bit) ^ 1) << bit
        partners.append(jnp.sum(got[pl.ds(first, 1 << bit)], axis=0))
    tiles = [partners[t] * (1.0 / math.sqrt(rank * rows * 2**t)) for t in range(levels)]
    low = lax.broadcasted_iota(jnp.int32, tiles[0].shape, 1) < rank
    tiles += [jnp.zeros_like(tiles[0])] * (levels % 2)
    turned = [pltpu.roll(tile, rank, 1) for tile in tiles]
    pairs = range(0, levels, 2)
    upper = jnp.concatenate([jnp.where(low, tiles[t], turned[t + 1]) for t in pairs], 1)
    lower = jnp.concatenate([jnp.where(low, turned[t], tiles[t + 1]) for t in pairs], 1)
    weights = jnp.concatenate([upper, lower], 0)[:, : levels * rank].astype(bases.dtype)
    far = contract(weights, bases[...].reshape(levels * rank, rows), (1, 0))
    full = image[...] + far
    shifted = masked(sizes, full - pull[...])
    shifted_ref[...] = shifted
    p = full.shape[0]
    half = p // 2
    shifted_parts = split(shifted, bases.dtype)
    full_parts = split(full, bases.dtype)
    left = jnp.concatenate([block[...]] + shifted_parts, 0)
    sums = jnp.zeros((4 * p, LANES), F32)
    for i in (2, 1, 0):
        own = block[...] if i == 0 else jnp.zeros_like(block[...])
        right = [shifted_parts[i], own, full_parts[i], shifted_parts[i]]
        sums = sums + contract(left, jnp.concatenate(right + right, 0), (1, 1))
    with_block = sums[:p]
    with_shifted = (sums[3 * p :] + sums[2 * p : 3 * p]) + sums[p : 2 * p]
    lane = lax.broadcasted_iota(jnp.int32, (half, LANES), 1)
    side = LANES // 2
    upper = jnp.where(lane < 3 * p, with_block[:half], with_shifted[:half])
    lower = jnp.where(lane < side + 3 * p, with_block[half:], with_shifted[half:])
    sums_ref[...] = jnp.where(lane < side, upper, lower)


def last_part(inverse, got, shifted, block, rayleigh_ref, factor_ref, next_ref):
    total = unfold(jnp.sum(got[...], axis=0)) * inverse
    p = total.shape[0]
    block_shifted = total[:, :p]
    block_block = total[:, p : 2 * p]
    rayleigh = total[:, 2 * p : 3 * p]
    corner = total[:, 3 * p :]
    rayleigh_ref[...] = rayleigh
    right = contract(block_block, rayleigh, (1, 0), HIGHEST) - block_shifted
    gram = corner + contract(
        jnp.concatenate([rayleigh, -block_shifted], 0),
        jnp.concatenate([right, rayleigh], 0),
        (0, 0),
        HIGHEST,
    )
    residual = shifted[...] - contract(rayleigh, block[...].astype(F32), (0, 0), HIGHEST)
    starts = range(0, residual.shape[1], LANES)
    parts = [residual[:, at : at + LANES] for at in starts]
    row = lax.broadcasted_iota(jnp.int32, (p, LANES), 0)
    lane = lax.broadcasted_iota(jnp.int32, (p, LANES), 1)
    columns = [jnp.broadcast_to(gram[:, k : k + 1], (p, LANES)) for k in range(p)]
    factor = jnp.zeros((p, LANES), F32)
    scale = jnp.zeros((p, LANES), F32)
    for k in range(p):
        pivot = jnp.broadcast_to(columns[k][k : k + 1, :], (p, LANES))
        root = lax.rsqrt(pivot)
        ratio = jnp.where(row > k, columns[k], 0.0) * (1.0 / pivot)
        factor = jnp.where(lane == k, jnp.where(row >= k, columns[k], 0.0) * root, factor)
        scale = jnp.where(row == k, root, scale)
        for j in range(k + 1, p):
            columns[j] = columns[j] - ratio * columns[j][k : k + 1, :]
        parts = [part - ratio * part[k : k + 1, :] for part in parts]
    factor_ref[...] = factor[:, :p]
    for at, part in zip(starts, parts):
        next_ref[:, at : at + LANES] = part * scale


def body(probes, previous, prev_coupling, leaves, bases, leaf_sizes):
    probe_count = probes.shape[0]
    levels, rank, rows = bases.shape
    chips = lax.axis_size(CHIPS)
    chip_bits = chips.bit_length() - 1
    devices = lax.axis_size(AXES)
    inverse = 1.0 / (devices * rows * 3 // 4)
    chip = chip_index().astype(jnp.int32).reshape(1)
    swap = [(0, 1), (1, 0)]
    tile = (probe_count // 2, 2 * rank)
    wide = jax.ShapeDtypeStruct((probe_count, rows), F32)
    square = jax.ShapeDtypeStruct((probe_count, probe_count), F32)
    keep = call(
        keep_mask,
        jax.ShapeDtypeStruct((8, rows), F32),
        [SMEM],
        flops=700000000,
        moved=0,
    )(leaf_sizes)
    partials, block = call(
        coefficients,
        (
            jax.ShapeDtypeStruct((levels,) + tile, F32),
            jax.ShapeDtypeStruct(probes.shape, probes.dtype),
        ),
        [VMEM] * 3,
        flops=2 * probe_count * levels * rank * rows,
        moved=2 * levels * rank * rows,
    )(keep, probes, bases)
    other = lax.ppermute(partials, CORE, swap)
    image, pull = call(
        own_part,
        (wide, wide),
        [VMEM] * 4,
        flops=2 * probe_count * rows * rows,
        moved=2 * rows * rows,
    )(block, leaves, previous, prev_coupling)
    other, image, pull = lax.optimization_barrier((other, image, pull))
    send = call(
        functools.partial(outgoing, chip_bits),
        jax.ShapeDtypeStruct((chips,) + tile, F32),
        [SMEM, VMEM, VMEM],
    )(chip, partials, other)
    got = lax.all_to_all(send, CHIPS, 0, 0, tiled=True)
    shifted, sums = call(
        functools.partial(coupled, chip_bits),
        (wide, jax.ShapeDtypeStruct((probe_count // 2, 8 * probe_count), F32)),
        [SMEM] * 2 + [VMEM] * 6,
    )(chip, leaf_sizes, got, other, bases, image, pull, block)
    sums = sums + lax.ppermute(sums, CORE, swap)
    spread = jnp.broadcast_to(sums[None], (chips,) + sums.shape)
    total = lax.all_to_all(spread, CHIPS, 0, 0, tiled=True)
    return call(
        functools.partial(last_part, inverse),
        (square, square, wide),
        [VMEM] * 3,
    )(total, shifted, block)


def solution(mesh):
    split = Mesh(mesh.devices.reshape(4, 4, 4, 2), AXES)
    return jax.shard_map(
        body,
        mesh=split,
        in_specs=(
            P(None, AXES),
            P(None, AXES),
            P(),
            P(AXES, None, None),
            P(None, None, AXES),
            P(AXES),
        ),
        out_specs=(P(), P(), P(None, AXES)),
        check_vma=False,
    )
```

```python
import functools
import math

import jax
import jax.numpy as jnp
from jax import lax
from jax.experimental import pallas as pl
from jax.experimental.pallas import tpu as pltpu
from jax.sharding import Mesh
from jax.sharding import PartitionSpec as P

AXES = ("gx_0", "gx_1", "gy_0", "gy_1")
CHIPS = ("gx_0", "gx_1", "gy_0")
CORE = "gy_1"
HIGHEST = lax.Precision.HIGHEST
VMEM = pl.BlockSpec(memory_space=pltpu.VMEM)
SMEM = pl.BlockSpec(memory_space=pltpu.SMEM)
LIMIT = 32 * 1024 * 1024
F32 = jnp.float32
LANES = 128


def fold(m):
    half = m.shape[-2] // 2
    return jnp.concatenate([m[..., :half, :], m[..., half:, :]], -1)


def unfold(m):
    half = m.shape[-1] // 2
    return jnp.concatenate([m[..., :half], m[..., half:]], -2)


def contract(a, b, over, precision=None):
    return lax.dot_general(
        a, b, ((over[:1], over[1:]), ((), ())), precision=precision, preferred_element_type=F32
    )


def split(x, dtype):
    parts = []
    for _ in range(3):
        parts.append(x.astype(dtype))
        x = x - parts[-1].astype(F32)
    return parts


def call(kernel, outs, ins, scratch=(), flops=0, moved=0):
    return pl.pallas_call(
        kernel,
        out_shape=outs,
        in_specs=ins,
        out_specs=jax.tree.map(lambda _: VMEM, outs),
        scratch_shapes=list(scratch),
        compiler_params=pltpu.CompilerParams(vmem_limit_bytes=LIMIT),
        cost_estimate=pl.CostEstimate(flops=flops, bytes_accessed=moved, transcendentals=0),
    )


def masked(sizes, raw):
    slot = lax.broadcasted_iota(jnp.int32, raw.shape, 1)
    return jnp.where(slot < sizes[0], raw.astype(F32), 0.0)


def keep_mask(sizes, keep_ref):
    slot = lax.broadcasted_iota(jnp.int32, keep_ref.shape, 1)
    keep_ref[...] = jnp.where(slot < sizes[0], 1.0, 0.0)


def coefficients(keep, probes, bases, out_ref, block_ref):
    levels, rank, rows = bases.shape
    block = jnp.where(keep[:1] > 0.0, probes[...].astype(F32), 0.0).astype(probes.dtype)
    block_ref[...] = block
    both = contract(block, bases[...].reshape(levels * rank, rows), (1, 1))
    for t in range(levels):
        out_ref[t] = fold(both[:, t * rank : (t + 1) * rank])


def own_part(block, leaf, previous, coupling, image_ref, pull_ref):
    image_ref[...] = contract(block[...], leaf[0], (1, 0))
    pull_ref[...] = contract(coupling[...], previous[...].astype(F32), (1, 0), HIGHEST)


def chip_index():
    index = 0
    for axis in CHIPS:
        index = index * lax.axis_size(axis) + lax.axis_index(axis)
    return index


def outgoing(chip_bits, chip_ref, own, other, out_ref):
    chip = chip_ref[0]
    out_ref[chip] = jnp.zeros(own.shape[1:], F32)
    for bit in range(chip_bits):
        first = ((chip >> bit) ^ 1) << bit
        mine = own[bit + 1] + other[bit + 1]
        out_ref[pl.ds(first, 1 << bit)] = jnp.broadcast_to(mine[None], (1 << bit,) + mine.shape)


def coupled(chip_bits, chip_ref, sizes, got, other, bases, image, pull, block, shifted_ref, sums_ref):
    levels, rank, rows = bases.shape
    chip = chip_ref[0]
    partners = [other[0]]
    for bit in range(chip_bits):
        first = ((chip >> bit) ^ 1) << bit
        partners.append(jnp.sum(got[pl.ds(first, 1 << bit)], axis=0))
    tiles = [partners[t] * (1.0 / math.sqrt(rank * rows * 2**t)) for t in range(levels)]
    low = lax.broadcasted_iota(jnp.int32, tiles[0].shape, 1) < rank
    tiles += [jnp.zeros_like(tiles[0])] * (levels % 2)
    turned = [pltpu.roll(tile, rank, 1) for tile in tiles]
    pairs = range(0, levels, 2)
    upper = jnp.concatenate([jnp.where(low, tiles[t], turned[t + 1]) for t in pairs], 1)
    lower = jnp.concatenate([jnp.where(low, turned[t], tiles[t + 1]) for t in pairs], 1)
    weights = jnp.concatenate([upper, lower], 0)[:, : levels * rank].astype(bases.dtype)
    far = contract(weights, bases[...].reshape(levels * rank, rows), (1, 0))
    full = image[...] + far
    shifted = masked(sizes, full - pull[...])
    shifted_ref[...] = shifted
    p = full.shape[0]
    half = p // 2
    shifted_parts = split(shifted, bases.dtype)
    full_parts = split(full, bases.dtype)
    left = jnp.concatenate([block[...]] + shifted_parts, 0)
    sums = jnp.zeros((4 * p, LANES), F32)
    for i in (2, 1, 0):
        own = block[...] if i == 0 else jnp.zeros_like(block[...])
        right = [shifted_parts[i], own, full_parts[i], shifted_parts[i]]
        sums = sums + contract(left, jnp.concatenate(right + right, 0), (1, 1))
    with_block = sums[:p]
    with_shifted = (sums[3 * p :] + sums[2 * p : 3 * p]) + sums[p : 2 * p]
    lane = lax.broadcasted_iota(jnp.int32, (half, LANES), 1)
    side = LANES // 2
    upper = jnp.where(lane < 3 * p, with_block[:half], with_shifted[:half])
    lower = jnp.where(lane < side + 3 * p, with_block[half:], with_shifted[half:])
    sums_ref[...] = jnp.where(lane < side, upper, lower)


def spread_out(own, other, out_ref):
    out_ref[...] = jnp.broadcast_to((own[...] + other[...])[None], out_ref.shape)


def last_part(inverse, got, shifted, block, rayleigh_ref, factor_ref, next_ref):
    total = unfold(jnp.sum(got[...], axis=0)) * inverse
    p = total.shape[0]
    block_shifted = total[:, :p]
    block_block = total[:, p : 2 * p]
    rayleigh = total[:, 2 * p : 3 * p]
    corner = total[:, 3 * p :]
    rayleigh_ref[...] = rayleigh
    right = contract(block_block, rayleigh, (1, 0), HIGHEST) - block_shifted
    gram = corner + contract(
        jnp.concatenate([rayleigh, -block_shifted], 0),
        jnp.concatenate([right, rayleigh], 0),
        (0, 0),
        HIGHEST,
    )
    residual = shifted[...] - contract(rayleigh, block[...].astype(F32), (0, 0), HIGHEST)
    half = p // 2
    tops = (0, half)
    starts = range(0, residual.shape[1], LANES)
    row = lax.broadcasted_iota(jnp.int32, (half, LANES), 0)
    lane = lax.broadcasted_iota(jnp.int32, (half, LANES), 1)
    columns = [
        [jnp.broadcast_to(gram[top : top + half, k : k + 1], (half, LANES)) for k in range(p)]
        for top in tops
    ]
    parts = [[residual[top : top + half, at : at + LANES] for at in starts] for top in tops]
    factor = [jnp.zeros((half, LANES), F32) for _ in tops]
    scale = [jnp.zeros((half, LANES), F32) for _ in tops]
    for k in range(p):
        side, at = divmod(k, half)
        here = slice(at, at + 1)
        pivot = jnp.broadcast_to(columns[side][k][here], (half, LANES))
        root = lax.rsqrt(pivot)
        reciprocal = 1.0 / pivot
        scale[side] = jnp.where(row == at, root, scale[side])
        for part in range(side, 2):
            column, ratio = columns[part][k], columns[part][k] * reciprocal
            if part == side:
                column = jnp.where(row >= at, column, 0.0)
                ratio = jnp.where(row > at, ratio, 0.0)
            factor[part] = jnp.where(lane == k, column * root, factor[part])
            if part == side and at == half - 1:
                continue
            for j in range(k + 1, p):
                columns[part][j] = columns[part][j] - ratio * columns[side][j][here]
            parts[part] = [x - ratio * y[here] for x, y in zip(parts[part], parts[side])]
    for part, top in enumerate(tops):
        factor_ref[top : top + half] = factor[part][:, :p]
        for at, x in zip(starts, parts[part]):
            next_ref[top : top + half, at : at + LANES] = x * scale[part]


def body(probes, previous, prev_coupling, leaves, bases, leaf_sizes):
    probe_count = probes.shape[0]
    levels, rank, rows = bases.shape
    chips = lax.axis_size(CHIPS)
    chip_bits = chips.bit_length() - 1
    devices = lax.axis_size(AXES)
    inverse = 1.0 / (devices * rows * 3 // 4)
    chip = chip_index().astype(jnp.int32).reshape(1)
    swap = [(0, 1), (1, 0)]
    tile = (probe_count // 2, 2 * rank)
    wide = jax.ShapeDtypeStruct((probe_count, rows), F32)
    square = jax.ShapeDtypeStruct((probe_count, probe_count), F32)
    keep = call(
        keep_mask,
        jax.ShapeDtypeStruct((8, rows), F32),
        [SMEM],
        flops=700000000,
        moved=0,
    )(leaf_sizes)
    partials, block = call(
        coefficients,
        (
            jax.ShapeDtypeStruct((levels,) + tile, F32),
            jax.ShapeDtypeStruct(probes.shape, probes.dtype),
        ),
        [VMEM] * 3,
        flops=2 * probe_count * levels * rank * rows,
        moved=2 * levels * rank * rows,
    )(keep, probes, bases)
    other = lax.ppermute(partials, CORE, swap)
    image, pull = call(
        own_part,
        (wide, wide),
        [VMEM] * 4,
        flops=2 * probe_count * rows * rows,
        moved=2 * rows * rows,
    )(block, leaves, previous, prev_coupling)
    other, image, pull = lax.optimization_barrier((other, image, pull))
    send = call(
        functools.partial(outgoing, chip_bits),
        jax.ShapeDtypeStruct((chips,) + tile, F32),
        [SMEM, VMEM, VMEM],
    )(chip, partials, other)
    got = lax.all_to_all(send, CHIPS, 0, 0, tiled=True)
    shifted, sums = call(
        functools.partial(coupled, chip_bits),
        (wide, jax.ShapeDtypeStruct((probe_count // 2, 8 * probe_count), F32)),
        [SMEM] * 2 + [VMEM] * 6,
    )(chip, leaf_sizes, got, other, bases, image, pull, block)
    spread = call(
        spread_out,
        jax.ShapeDtypeStruct((chips,) + sums.shape, F32),
        [VMEM] * 2,
    )(sums, lax.ppermute(sums, CORE, swap))
    total = lax.all_to_all(spread, CHIPS, 0, 0, tiled=True)
    return call(
        functools.partial(last_part, inverse),
        (square, square, wide),
        [VMEM] * 3,
    )(total, shifted, block)


def solution(mesh):
    split = Mesh(mesh.devices.reshape(4, 4, 4, 2), AXES)
    return jax.shard_map(
        body,
        mesh=split,
        in_specs=(
            P(None, AXES),
            P(None, AXES),
            P(),
            P(AXES, None, None),
            P(None, None, AXES),
            P(AXES),
        ),
        out_specs=(P(), P(), P(None, AXES)),
        check_vma=False,
    )
```
